32 devices in a mesh: grp: 2 (over y), dp: 4 (over z), sub: 2 (over x), rep: 2 (over core).
Axes of the slice: x: 2, y: 2, z: 4, core: 2. Of those that a mesh axis runs over, the one named last changes fastest.
Arguments:
- fine: bfloat16 [16, 32, 16, 16, 128], P(('grp', 'dp', 'rep'), 'sub'), parts along dimension 0, may hold values from -6 to 6
- conv_weight: bfloat16 [27, 128, 128], replicated, may hold values from -0.109375 to 0.109375
- query_weight: bfloat16 [128, 512], replicated, may hold values from -0.5 to 0.5
- out_weight: bfloat16 [512, 128], replicated, may hold values from -0.25 to 0.25
- coarse_kv: bfloat16 [8, 64, 2, 8, 512], P(('grp', 'sub', 'rep'), 'dp'), parts along dimension 0, may hold values from -6 to 6
- key_bias: bfloat16 [8, 64, 8], P(('grp', 'sub', 'rep'), 'dp'), parts along dimension 0, may hold values from -2 to 303
- zone_ids: int32 [16, 2, 16], P(('grp', 'dp', 'rep'), 'sub'), parts along dimension 0, may hold values from 0 to 63, as said below
- zone_counts: int32 [16, 2], P(('grp', 'dp', 'rep'), 'sub'), parts along dimension 0, may hold values from 8 to 16
- grad_out: bfloat16 [16, 16, 8, 8, 128], P(('grp', 'dp', 'rep'), 'sub'), parts along dimension 0, may hold values from -6 to 6
Outputs:
- weight_grads: float32 [1146880], P(('grp', 'dp', 'sub', 'rep')), parts along dimension 0
- coarse_grad: float32 [8, 64, 2, 8, 512], P(('grp', 'sub', 'rep'), 'dp'), parts along dimension 0
The draws below stay inside these ranges and needn't reach their ends.
There are 2 independent parts, one for each index of `grp`. The reference program is written for one: setup_inputs(seed, part) draws one part's arguments, and reference() takes and returns one part's arrays. A program takes and returns all parts, laid end to end along the dimension named above; an argument that names none is the same for every part. Nothing has to cross between parts.
Inputs may be any that keep to these rules, and one draw needn't show every extreme that they name: `zone_ids`: among all 16 entries of the lists of the 1 patches at positions s .. s + 1 - 1 of one track (used or not), at most 8 entries lie in one block of 16 consecutive tile numbers; in every lane one block is named exactly 8 times by each such group of patches of that lane.
All inputs are finite; a program needn't handle non-finite values.
Results may differ from the reference program's by a relative error of at most 0.0058.
Values may be sent and summed in bfloat16 or wider, within the bound.
A program may use at most 64 MiB of HBM per device.

```python
import jax
import jax.numpy as jnp
from jax import lax

CHANNELS = 128
HEADS = 8
HEAD_DIM = 64
EDGE = 16
TILE_KEYS = 8
TILE_DEV = 16
LIST_LEN = 16
PATCH_DEV = 1
INNER = 512
OUT_EDGE = 8
TRACKS = 8
REP_TRACKS = 2
SEG_PATCHES = 2
STRIP = 32
LANES = 4
TILES = 64
CAPACITY = 8


def draw_zone_ids(key, part):
    dp_count = TILES // TILE_DEV
    sub_count = LANES // REP_TRACKS
    slot_count = PATCH_DEV * LIST_LEN
    hot_owner = jax.random.randint(jax.random.fold_in(key, 11), (LANES,), 0, dp_count)

    def one_device(device):
        lane = device % LANES
        hot = hot_owner[lane]
        device_key = jax.random.fold_in(jax.random.fold_in(key, 12), device)
        key_a, key_b, key_c = jax.random.split(device_key, 3)
        spread = jnp.arange((dp_count - 1) * CAPACITY, dtype=jnp.int32) // CAPACITY
        others = (hot + 1 + spread) % dp_count
        others = jax.random.permutation(key_a, others)
        owners = jnp.concatenate([jnp.full((CAPACITY,), hot, jnp.int32), others[:slot_count - CAPACITY]])
        owners = jax.random.permutation(key_b, owners)
        local_idx = jax.random.randint(key_c, (slot_count,), 0, TILE_DEV)
        return (owners * TILE_DEV + local_idx).reshape(PATCH_DEV, LIST_LEN)
    every_list = jax.vmap(one_device)(jnp.arange(dp_count * LANES, dtype=jnp.int32))
    every_list = every_list.reshape(dp_count, sub_count, REP_TRACKS, PATCH_DEV, LIST_LEN)
    every_list = jnp.transpose(every_list, (0, 2, 1, 3, 4))
    return every_list.reshape(TRACKS, SEG_PATCHES, LIST_LEN)


def draw_zone_counts(key, part):
    counts = jax.random.randint(jax.random.fold_in(key, 21), (TRACKS, SEG_PATCHES), LIST_LEN // 2, LIST_LEN + 1)
    row_pick = jax.random.randint(jax.random.fold_in(key, 22), (), 0, TRACKS)
    col_pick = jax.random.randint(jax.random.fold_in(key, 23), (), 0, SEG_PATCHES)
    return counts.at[row_pick, col_pick].set(LIST_LEN)


def draw_key_bias(key, part):
    shape = (LANES, TILES, TILE_KEYS)
    key_c = jax.random.fold_in(jax.random.fold_in(key, 31), 2)
    values = jax.random.uniform(key_c, shape, jnp.float32, -2.0, 2.0)
    return values.astype(jnp.bfloat16)


def levels(key, extent, shards, least, top_value):
    level = 1.0
    for dim, blocks in shards:
        draws = jax.random.uniform(jax.random.fold_in(jax.random.fold_in(key, 6), dim), (blocks,), jnp.float32, least / len(shards), top_value / len(shards))
        level = level * jnp.repeat(jnp.exp(draws), extent[dim] // blocks).reshape((-1,) + (1,) * (len(extent) - 1 - dim))
    return level


def gaussian(key, shape, scale, most, cuts=(), held_as=jnp.bfloat16):
    gain = levels(key, shape, cuts, -0.22, 0.18) if cuts else 1.0
    values = jax.random.normal(key, shape, jnp.float32) * scale * gain
    return jnp.minimum(jnp.maximum(values, -most), most).astype(held_as)


def setup_inputs(seed: int = 0, part: int = 0) -> dict:
    key_of = jax.random.split(jax.random.key(seed), 10)
    part_keys = jax.random.split(jax.random.fold_in(key_of[9], part), 10)
    fine = gaussian(part_keys[0], (TRACKS, STRIP, EDGE, EDGE, CHANNELS), 1.0, 6.0, ((0, 8), (1, 2)))
    conv_weight = gaussian(key_of[1], (27, CHANNELS, CHANNELS), (27 * CHANNELS) ** -0.5, 0.109375)
    query_weight = gaussian(key_of[2], (CHANNELS, INNER), CHANNELS ** -0.5, 0.5)
    out_weight = gaussian(key_of[3], (INNER, CHANNELS), INNER ** -0.5, 0.25)
    coarse_kv = gaussian(part_keys[4], (LANES, TILES, 2, TILE_KEYS, INNER), 1.0, 6.0, ((0, 4), (1, 4)))
    key_bias = draw_key_bias(jax.random.fold_in(jax.random.fold_in(key_of[9], part), 71), part)
    zone_ids = draw_zone_ids(jax.random.fold_in(jax.random.fold_in(key_of[9], part), 71), part)
    zone_counts = draw_zone_counts(jax.random.fold_in(jax.random.fold_in(key_of[9], part), 71), part)
    grad_out = gaussian(part_keys[8], (TRACKS, OUT_EDGE * SEG_PATCHES, OUT_EDGE, OUT_EDGE, CHANNELS), 1.0, 6.0, ((0, 8), (1, 2)))
    return dict(fine=fine, conv_weight=conv_weight, query_weight=query_weight, out_weight=out_weight, coarse_kv=coarse_kv, key_bias=key_bias, zone_ids=zone_ids, zone_counts=zone_counts, grad_out=grad_out)


def silu_grad(value):
    sig = jax.nn.sigmoid(value)
    return sig * (1.0 + value * (1.0 - sig))

def rounded(value):
    return lax.optimization_barrier(value.astype(jnp.bfloat16)).astype(jnp.float32)

def strided_columns(padded):
    strip_len = padded.shape[0] - 1
    side_len = padded.shape[1] - 1
    channels = padded.shape[3]
    pieces = []
    for off_x in range(3):
        for off_y in range(3):
            for off_z in range(3):
                pieces.append(lax.slice(padded, (off_x, off_y, off_z, 0), (off_x + strip_len - 1, off_y + side_len - 1, off_z + side_len - 1, channels), (2, 2, 2, 1)))
    stacked = jnp.concatenate(pieces, axis=3)
    return stacked.reshape(-1, stacked.shape[3])

def track_columns(strip_cells):
    return strided_columns(jnp.pad(strip_cells, ((1, 0), (1, 0), (1, 0), (0, 0))))

def reference(fine, conv_weight, query_weight, out_weight, coarse_kv, key_bias, zone_ids, zone_counts, grad_out):
    conv_mat = conv_weight.reshape(27 * CHANNELS, CHANNELS)

    def forward_track(strip_cells):
        return jnp.dot(track_columns(strip_cells), conv_mat, preferred_element_type=jnp.float32)
    pre_act = lax.map(forward_track, fine)
    features = jax.nn.silu(pre_act).astype(jnp.bfloat16)
    patch_total = TRACKS * SEG_PATCHES
    patch_rows = OUT_EDGE ** 3
    feat_patch = features.reshape(patch_total, patch_rows, CHANNELS)
    upstream = grad_out.reshape(patch_total, patch_rows, CHANNELS)
    id_lists = zone_ids.reshape(patch_total, LIST_LEN)
    count_list = zone_counts.reshape(patch_total)
    patch_index = jnp.arange(patch_total, dtype=jnp.int32)
    track_of = patch_index // SEG_PATCHES
    place_of = patch_index % SEG_PATCHES
    lane_of = place_of // PATCH_DEV * REP_TRACKS + track_of % REP_TRACKS
    coarse_full = coarse_kv.astype(jnp.float32)
    bias_full = key_bias.astype(jnp.float32)

    def per_patch(carry, items):
        grad_query_w, grad_out_w, coarse_grad = carry
        feat_one, up_one, ids_one, count_one, lane_one = items
        tiles = coarse_full[lane_one, ids_one]
        key_rows = tiles[:, 0].reshape(LIST_LEN * TILE_KEYS, HEADS, HEAD_DIM)
        value_rows = tiles[:, 1].reshape(LIST_LEN * TILE_KEYS, HEADS, HEAD_DIM)
        bias_row = bias_full[lane_one, ids_one].reshape(-1)
        live = jnp.repeat(jnp.arange(LIST_LEN, dtype=jnp.int32) < count_one, TILE_KEYS)
        queries = jnp.dot(feat_one, query_weight, preferred_element_type=jnp.float32).astype(jnp.bfloat16)
        query_full = queries.astype(jnp.float32).reshape(patch_rows, HEADS, HEAD_DIM)
        scores = jnp.einsum('qhd,khd->hqk', query_full, key_rows) * 0.125 + bias_row[None, None, :]
        scores = jnp.where(live[None, None, :], scores, -jnp.inf)
        row_max = lax.optimization_barrier(jnp.max(scores, axis=-1, keepdims=True))
        exps = jnp.exp(scores - row_max)
        attn_prob = exps / lax.optimization_barrier(jnp.sum(exps, axis=-1, keepdims=True))
        prob_bf = rounded(attn_prob)
        attended = rounded(jnp.einsum('hqk,khd->qhd', prob_bf, value_rows)).reshape(patch_rows, INNER)
        attended_bf = attended.astype(jnp.bfloat16)
        grad_out_w = grad_out_w + jnp.dot(attended_bf.T, up_one, preferred_element_type=jnp.float32)
        grad_attended = rounded(jnp.dot(up_one, out_weight.T, preferred_element_type=jnp.float32)).reshape(patch_rows, HEADS, HEAD_DIM)
        grad_prob = jnp.einsum('qhd,khd->hqk', grad_attended, value_rows)
        grad_values = rounded(jnp.einsum('hqk,qhd->khd', prob_bf, grad_attended))
        row_dot = lax.optimization_barrier(jnp.sum(attn_prob * grad_prob, axis=-1, keepdims=True))
        grad_scores = rounded(attn_prob * (grad_prob - row_dot))
        grad_queries = rounded(jnp.einsum('hqk,khd->qhd', grad_scores, key_rows) * 0.125).reshape(patch_rows, INNER)
        grad_keys = rounded(jnp.einsum('hqk,qhd->khd', grad_scores, query_full) * 0.125)
        grad_q_bf = grad_queries.astype(jnp.bfloat16)
        grad_query_w = grad_query_w + jnp.dot(feat_one.T, grad_q_bf, preferred_element_type=jnp.float32)
        grad_features = up_one.astype(jnp.float32) + jnp.dot(grad_q_bf, query_weight.T, preferred_element_type=jnp.float32)
        tile_grad = jnp.stack([grad_keys.reshape(LIST_LEN, TILE_KEYS, INNER), grad_values.reshape(LIST_LEN, TILE_KEYS, INNER)], axis=1)
        coarse_grad = coarse_grad.at[lane_one, ids_one].add(tile_grad)
        return ((grad_query_w, grad_out_w, coarse_grad), grad_features)
    start = (jnp.zeros((CHANNELS, INNER), jnp.float32), jnp.zeros((INNER, CHANNELS), jnp.float32), jnp.zeros((LANES, TILES, 2, TILE_KEYS, INNER), jnp.float32))
    (grad_query_w, grad_out_w, coarse_grad), grad_features = lax.scan(per_patch, start, (feat_patch, upstream, id_lists, count_list, lane_of))
    grad_features = grad_features.reshape(pre_act.shape)
    grad_pre = (grad_features * silu_grad(pre_act)).astype(jnp.bfloat16)

    def weight_track(total, items):
        strip_cells, grad_rows = items
        return (total + jnp.dot(track_columns(strip_cells).T, grad_rows, preferred_element_type=jnp.float32), None)
    grad_conv_w, unused = lax.scan(weight_track, jnp.zeros((27 * CHANNELS, CHANNELS), jnp.float32), (fine, grad_pre))
    weight_grads = jnp.concatenate([grad_conv_w.reshape(-1), grad_query_w.reshape(-1), grad_out_w.reshape(-1)])
    return (weight_grads, coarse_grad)
```

```python
import functools

import jax
import jax.numpy as jnp
import numpy as np
from jax import lax
from jax.experimental import pallas as pl
from jax.experimental.pallas import tpu as pltpu
from jax.sharding import PartitionSpec as P

HEADS = 8
MESH = pl.DeviceIdType.MESH
F32 = jnp.float32
BF16 = jnp.bfloat16


def dot(a, b):
    return jnp.dot(a, b, preferred_element_type=F32)


def dot_nt(a, b):
    return lax.dot_general(a, b, (((1,), (1,)), ((), ())), preferred_element_type=F32)


def dot_tn(a, b):
    return lax.dot_general(a, b, (((0,), (0,)), ((), ())), preferred_element_type=F32)


def iota(shape, dim):
    return lax.broadcasted_iota(jnp.int32, shape, dim)


def tap_selector(side):
    half = side // 2
    sel = np.zeros((9, half, half, side, side), np.float32)
    for b in range(3):
        for c in range(3):
            for y in range(half):
                for z in range(half):
                    yy, zz = 2 * y + b - 1, 2 * z + c - 1
                    if yy >= 0 and zz >= 0:
                        sel[b * 3 + c, y, z, yy, zz] = 1.0
    return sel.reshape(9 * half * half, side * side)


def kernel(
    cfg,
    fine,
    selector,
    conv_w,
    query_w,
    out_w,
    kv,
    meta,
    upstream,
    weight_out,
    tile_out,
    halo,
    t_even,
    t_odd,
    pre,
    feat,
    query,
    grad_att,
    grad_kv,
    grad_query,
    acc,
    metas,
    kv_send,
    kv_recv,
    slot_send,
    slot_recv,
    picks,
    rep_send,
    rep_recv,
    sub_send,
    sub_recv,
    part,
    dp_send,
    dp_recv,
    halo_sem,
    meta_sem,
    kv_sem,
    slot_sem,
    rep_sem,
    sub_sem,
    dp_sem,
):
    dps, subs, tiles, cap, slots, rows_dev, reduce_here = cfg
    me = lax.axis_index("dp")
    sub = lax.axis_index("sub")
    rep = lax.axis_index("rep")
    cap_rows = cap * 16
    planes = t_even.shape[0]
    cells = t_even.shape[1]
    channels = fine.shape[2]
    lanes = slots * 8
    peers = [lax.rem(me + d, dps) for d in range(dps)]
    behind = [lax.rem(me + dps - d, dps) for d in range(dps)]

    barrier = pltpu.get_barrier_semaphore()
    greeted = 0
    for d in range(1, dps):
        pl.semaphore_signal(barrier, inc=1, device_id={"dp": peers[d]}, device_id_type=MESH)
        greeted += 1
    for step in (1, subs - 1) if subs > 2 else (1,):
        pl.semaphore_signal(
            barrier, inc=1, device_id={"sub": lax.rem(sub + step, subs)}, device_id_type=MESH
        )
        greeted += 1
    pl.semaphore_signal(barrier, inc=1, device_id={"rep": 1 - rep}, device_id_type=MESH)
    greeted += 1
    pl.semaphore_wait(barrier, greeted)

    def send(src, dst, sems, index, where):
        return pltpu.make_async_remote_copy(
            src_ref=src,
            dst_ref=dst,
            send_sem=sems.at[0, index],
            recv_sem=sems.at[1, index],
            device_id=where,
            device_id_type=MESH,
        )

    meta_copies = [
        send(meta, metas.at[me], meta_sem, d, {"dp": peers[d]}) for d in range(1, dps)
    ]
    for copy in meta_copies:
        copy.start()
    halo_copy = send(
        fine.at[2 * planes - 1], halo, halo_sem, 0, {"sub": lax.rem(sub + 1, subs)}
    )
    halo_copy.start()
    metas[me] = meta[...]

    def spread_taps(found, target, index):
        for tap in range(9):
            target[index, :, tap * channels : (tap + 1) * channels] = found[
                tap * cells : (tap + 1) * cells
            ]

    def unfold(i, carry):
        pair = jnp.concatenate([fine[2 * i], fine[2 * i + 1]], axis=1)
        found = dot(selector[...], pair).astype(BF16)
        spread_taps(found[:, :channels], t_even, i)
        spread_taps(found[:, channels:], t_odd, i + 1)
        return carry

    lax.fori_loop(0, planes, unfold, 0)

    for copy in meta_copies:
        copy.wait()

    def slot_dest(ids_row):
        owner_row = jnp.floor(ids_row * (1.0 / tiles))
        owner_col = jnp.transpose(jnp.broadcast_to(owner_row, (lanes, lanes)))
        earlier = (iota((lanes, lanes), 0) // 8) < (iota((lanes, lanes), 1) // 8)
        same = jnp.where((owner_col == owner_row) & earlier, 1.0, 0.0)
        rank = jnp.sum(same, axis=0, keepdims=True) * 0.125
        return owner_row * cap + rank

    me_f = me.astype(F32)

    def picker(ids_row):
        dest = slot_dest(ids_row)
        slot_row = (iota((cap_rows, lanes), 0) // 16).astype(F32) + me_f * cap
        first = (iota((cap_rows, lanes), 1) % 8) == 0
        by_slot = jnp.where((slot_row == dest) & first, 1.0, 0.0).astype(BF16)
        tile_row = (iota((tiles * 16, lanes), 0) // 16).astype(F32) + me_f * tiles
        by_tile = jnp.where(tile_row == ids_row, 1.0, 0.0).astype(BF16)
        matched = dot_nt(by_slot, by_tile)
        unit = (iota(matched.shape, 0) % 16) == (iota(matched.shape, 1) % 16)
        return jnp.where(unit, matched, 0.0).astype(BF16)

    kv_copies = []
    for d in range(dps - 1, -1, -1):
        ids_row = metas[peers[d], tiles : tiles + 1, :]
        pick = picker(ids_row)
        picks[peers[d]] = pick
        chosen = dot(pick, kv[...]).astype(BF16)
        if d == 0:
            kv_recv[me] = chosen
        else:
            kv_send[d - 1] = chosen
            copy = send(kv_send.at[d - 1], kv_recv.at[me], kv_sem, d, {"dp": peers[d]})
            copy.start()
            kv_copies.append(copy)

    halo_copy.wait()
    edge = dot(selector[...], halo[...])
    edge = jnp.where(sub > 0, edge, 0.0).astype(BF16)
    spread_taps(edge, t_odd, 0)

    row_count = planes * cells

    def columns(a):
        if a == 1:
            return t_even[...].reshape(row_count, 9 * channels)
        start = a // 2
        return t_odd[start : start + planes].reshape(row_count, 9 * channels)

    value = dot(columns(0), conv_w[0]) + dot(columns(1), conv_w[1]) + dot(columns(2), conv_w[2])
    pre[...] = value
    feat[...] = (value * jax.nn.sigmoid(value)).astype(BF16)
    query[...] = dot(feat[...], query_w[...]).astype(BF16)
    grad_att[...] = dot_nt(upstream[...], out_w[...]).astype(BF16)

    ids_row = meta[tiles : tiles + 1, :]
    count = meta[tiles + 1 : tiles + 2, :]
    dest = slot_dest(ids_row)
    dest2 = jnp.concatenate([dest, dest], axis=1)
    place_rows = dps * cap_rows
    row_i = iota((place_rows, 2 * lanes), 0)
    lane_i = iota((place_rows, 2 * lanes), 1)
    fits = ((row_i // 16).astype(F32) == dest2) & (
        (row_i % 16) == (lane_i // lanes) * 8 + lane_i % 8
    )
    placing = jnp.where(fits, 1.0, 0.0).astype(BF16)

    bias = jnp.zeros((1, lanes), F32)
    for owner in range(dps):
        tile_row = iota((tiles, lanes), 0).astype(F32) + float(owner * tiles)
        bias = bias + jnp.sum(
            jnp.where(tile_row == ids_row, metas[owner, :tiles, :], 0.0), axis=0, keepdims=True
        )
    lane_slot = (iota((1, lanes), 1) // 8).astype(F32)
    live = lane_slot < count
    bias = jnp.where(live, bias, -jnp.inf)

    for copy in kv_copies:
        copy.wait()
    kv_all = dot_tn(placing, kv_recv[...].reshape(place_rows, kv.shape[1])).astype(BF16)

    low = iota((lanes, 128), 1) < 64
    conv_rows = 27 * channels
    pairs = query.shape[1] // 128
    for j in range(pairs):
        cut = slice(j * 128, (j + 1) * 128)
        keys = kv_all[:lanes, cut]
        values = kv_all[lanes:, cut]
        none = jnp.zeros_like(keys)
        keys2 = jnp.concatenate(
            [jnp.where(low, keys, none), jnp.where(low, none, keys)], axis=0
        )
        values2 = jnp.concatenate(
            [jnp.where(low, values, none), jnp.where(low, none, values)], axis=0
        )
        q = query[:, cut]
        g = grad_att[:, cut]
        scores = dot_nt(q, keys2) * 0.125
        probs = []
        for h in range(2):
            s = scores[:, h * lanes : (h + 1) * lanes] + bias
            e = jnp.exp(s - jnp.max(s, axis=1, keepdims=True))
            probs.append(e / jnp.sum(e, axis=1, keepdims=True))
        prob_b = jnp.concatenate([p.astype(BF16) for p in probs], axis=1)
        attended = dot(prob_b, values2).astype(BF16)
        acc[conv_rows + 512 * channels // 128 + j * 128 : conv_rows + 512 * channels // 128 + (j + 1) * 128, :] = dot_tn(
            attended, upstream[...]
        )
        grad_prob = dot_nt(g, values2)
        gs = []
        for h in range(2):
            gp = grad_prob[:, h * lanes : (h + 1) * lanes]
            gs.append(
                (probs[h] * (gp - jnp.sum(probs[h] * gp, axis=1, keepdims=True))).astype(BF16)
            )
        grad_s = jnp.concatenate(gs, axis=1)
        gv = dot_tn(prob_b, g)
        grad_kv[lanes:, cut] = jnp.where(low, gv[:lanes], gv[lanes:]).astype(BF16)
        gk = dot_tn(grad_s, q) * 0.125
        grad_kv[:lanes, cut] = jnp.where(low, gk[:lanes], gk[lanes:]).astype(BF16)
        gq = (dot(grad_s, keys2) * 0.125).astype(BF16)
        grad_query[:, cut] = gq
        acc[pl.ds(conv_rows + j, channels, stride=pairs), :] = dot_tn(feat[...], gq)

    outgoing = dot(placing, grad_kv[...]).astype(BF16)
    slot_send[...] = outgoing.reshape(dps, cap_rows, kv.shape[1])
    slot_copies = []
    for d in range(dps - 1, 0, -1):
        copy = send(slot_send.at[peers[d]], slot_recv.at[me], slot_sem, d, {"dp": peers[d]})
        copy.start()
        slot_copies.append(copy)
    slot_recv[me] = slot_send[me]

    grad_feat = upstream[...].astype(F32) + dot_nt(grad_query[...], query_w[...])
    v = pre[...]
    sig = jax.nn.sigmoid(v)
    grad_pre = (grad_feat * (sig * (1.0 + v * (1.0 - sig)))).astype(BF16)
    for a in range(3):
        acc[a * 9 * channels : (a + 1) * 9 * channels, :] = dot_tn(columns(a), grad_pre)

    if reduce_here:
        pad_rows = rep_send.shape[2]
        acc[acc.shape[0] - 8 :, :] = jnp.zeros((8, 128), F32)

        def chunk(p, s, r):
            start = pl.multiple_of(((p * subs + s) * 2 + r) * rows_dev, 8)
            return acc[pl.ds(start, pad_rows), :]

        rep_copies = []
        for half in range(2):
            s = (1 - sub) if half == 0 else sub
            for p in range(dps):
                rep_send[half, p] = chunk(p, s, 1 - rep).astype(BF16)
            copy = send(rep_send.at[half], rep_recv.at[half], rep_sem, half, {"rep": 1 - rep})
            copy.start()
            rep_copies.append(copy)
        rep_copies[0].wait()
        for p in range(dps):
            sub_send[p] = (chunk(p, 1 - sub, rep) + rep_recv[0, p].astype(F32)).astype(BF16)
        sub_copy = send(sub_send, sub_recv, sub_sem, 0, {"sub": 1 - sub})
        sub_copy.start()
        rep_copies[1].wait()
        for p in range(dps):
            part[p] = chunk(p, sub, rep) + rep_recv[1, p].astype(F32)
        sub_copy.wait()
        dp_copies = []
        for d in range(dps - 1, 0, -1):
            p = peers[d]
            dp_send[d - 1] = (part[p] + sub_recv[p].astype(F32)).astype(BF16)
            copy = send(dp_send.at[d - 1], dp_recv.at[d - 1], dp_sem, d, {"dp": p})
            copy.start()
            dp_copies.append(copy)
        total = part[me] + sub_recv[me].astype(F32)

    for copy in slot_copies:
        copy.wait()
    tile_out[...] = dot_tn(
        picks[...].reshape(place_rows, tiles * 16),
        slot_recv[...].reshape(place_rows, kv.shape[1]),
    )
    if reduce_here:
        for copy in dp_copies:
            copy.wait()
        for d in range(1, dps):
            total = total + dp_recv[d - 1].astype(F32)
        weight_out[...] = total[:rows_dev]
    else:
        weight_out[...] = acc[: weight_out.shape[0], :]


def per_device(
    fine,
    conv_weight,
    query_weight,
    out_weight,
    coarse_kv,
    key_bias,
    zone_ids,
    zone_counts,
    grad_out,
):
    strip_len, side, _, channels = fine.shape[1:]
    inner = query_weight.shape[1]
    tiles = coarse_kv.shape[1]
    slots = zone_ids.shape[1] * zone_ids.shape[2]
    dps, subs, reps = lax.axis_size("dp"), lax.axis_size("sub"), lax.axis_size("rep")
    cap = 2 * slots // dps
    cap_rows = cap * 16
    lanes = slots * 8
    planes = strip_len // 2
    cells = (side // 2) ** 2
    rows = planes * cells
    weight_rows = (27 * channels * channels + 2 * channels * inner) // 128
    devices = dps * subs * reps
    reduce_here = subs == 2 and weight_rows % (8 * devices) == 0
    rows_dev = weight_rows // devices if reduce_here else 16
    pad_rows = -(-rows_dev // 16) * 16
    bias_rows = jnp.tile(key_bias[0].astype(F32), (1, slots))
    ids_row = jnp.repeat(zone_ids[0].reshape(-1), 8).astype(F32)
    count_row = jnp.full((1, lanes), zone_counts[0, 0], F32)
    meta = jnp.concatenate(
        [bias_rows, ids_row[None], jnp.broadcast_to(count_row, (7, lanes))], axis=0
    )
    cfg = (dps, subs, tiles, cap, slots, rows_dev, reduce_here)
    weight_shape = (rows_dev, 128) if reduce_here else (weight_rows, 128)
    vmem = pl.BlockSpec(memory_space=pltpu.VMEM)
    weight_out, tile_out = pl.pallas_call(
        functools.partial(kernel, cfg),
        out_shape=(
            jax.ShapeDtypeStruct(weight_shape, F32),
            jax.ShapeDtypeStruct((tiles * 16, inner), F32),
        ),
        in_specs=[vmem] * 8,
        out_specs=(vmem, vmem),
        scratch_shapes=[
            pltpu.VMEM((side * side, channels), BF16),
            pltpu.VMEM((planes, cells, 9 * channels), BF16),
            pltpu.VMEM((planes + 1, cells, 9 * channels), BF16),
            pltpu.VMEM((rows, channels), F32),
            pltpu.VMEM((rows, channels), BF16),
            pltpu.VMEM((rows, inner), BF16),
            pltpu.VMEM((rows, inner), BF16),
            pltpu.VMEM((2 * lanes, inner), BF16),
            pltpu.VMEM((rows, inner), BF16),
            pltpu.VMEM((weight_rows + 8, 128), F32),
            pltpu.VMEM((dps, tiles + 8, lanes), F32),
            pltpu.VMEM((dps - 1, cap_rows, inner), BF16),
            pltpu.VMEM((dps, cap_rows, inner), BF16),
            pltpu.VMEM((dps, cap_rows, inner), BF16),
            pltpu.VMEM((dps, cap_rows, inner), BF16),
            pltpu.VMEM((dps, cap_rows, tiles * 16), BF16),
            pltpu.VMEM((2, dps, pad_rows, 128), BF16),
            pltpu.VMEM((2, dps, pad_rows, 128), BF16),
            pltpu.VMEM((dps, pad_rows, 128), BF16),
            pltpu.VMEM((dps, pad_rows, 128), BF16),
            pltpu.VMEM((dps, pad_rows, 128), F32),
            pltpu.VMEM((dps - 1, pad_rows, 128), BF16),
            pltpu.VMEM((dps - 1, pad_rows, 128), BF16),
            pltpu.SemaphoreType.DMA((2, 1)),
            pltpu.SemaphoreType.DMA((2, dps)),
            pltpu.SemaphoreType.DMA((2, dps)),
            pltpu.SemaphoreType.DMA((2, dps)),
            pltpu.SemaphoreType.DMA((2, 2)),
            pltpu.SemaphoreType.DMA((2, 1)),
            pltpu.SemaphoreType.DMA((2, dps)),
        ],
        compiler_params=pltpu.CompilerParams(
            collective_id=0, has_side_effects=True, vmem_limit_bytes=48 * 1024 * 1024
        ),
    )(
        fine[0].reshape(strip_len, side * side, channels),
        jnp.asarray(tap_selector(side), BF16),
        conv_weight.reshape(3, 9 * channels, channels),
        query_weight,
        out_weight,
        coarse_kv[0].reshape(tiles * 16, inner),
        meta,
        grad_out[0].reshape(rows, channels),
    )
    weight_grads = weight_out.reshape(-1)
    if not reduce_here:
        weight_grads = lax.psum_scatter(
            weight_grads, ("dp", "sub", "rep"), scatter_dimension=0, tiled=True
        )
    return (weight_grads, tile_out.reshape(1, tiles, 2, 8, inner))


def solution(mesh):
    in_specs = (
        P(("grp", "dp", "rep"), "sub", None, None, None),
        P(),
        P(),
        P(),
        P(("grp", "sub", "rep"), "dp", None, None, None),
        P(("grp", "sub", "rep"), "dp", None),
        P(("grp", "dp", "rep"), "sub", None),
        P(("grp", "dp", "rep"), "sub"),
        P(("grp", "dp", "rep"), "sub", None, None, None),
    )
    out_specs = (P(("grp", "dp", "sub", "rep")), P(("grp", "sub", "rep"), "dp", None, None, None))
    return jax.shard_map(
        per_device, mesh=mesh, in_specs=in_specs, out_specs=out_specs, check_vma=False
    )
```

```python
import functools

import jax
import jax.numpy as jnp
import numpy as np
from jax import lax
from jax.experimental import pallas as pl
from jax.experimental.pallas import tpu as pltpu
from jax.sharding import PartitionSpec as P

HEADS = 8
MESH = pl.DeviceIdType.MESH
F32 = jnp.float32
BF16 = jnp.bfloat16


def dot(a, b):
    return jnp.dot(a, b, preferred_element_type=F32)


def dot_nt(a, b):
    return lax.dot_general(a, b, (((1,), (1,)), ((), ())), preferred_element_type=F32)


def dot_tn(a, b):
    return lax.dot_general(a, b, (((0,), (0,)), ((), ())), preferred_element_type=F32)


def iota(shape, dim):
    return lax.broadcasted_iota(jnp.int32, shape, dim)


def tap_selector(side):
    half = side // 2
    sel = np.zeros((9, half, half, side, side), np.float32)
    for b in range(3):
        for c in range(3):
            for y in range(half):
                for z in range(half):
                    yy, zz = 2 * y + b - 1, 2 * z + c - 1
                    if yy >= 0 and zz >= 0:
                        sel[b * 3 + c, y, z, yy, zz] = 1.0
    return sel.reshape(9 * half * half, side * side)


def kernel(
    cfg,
    fine_hbm,
    selector_hbm,
    conv_w_hbm,
    query_w_hbm,
    out_w_hbm,
    kv_hbm,
    bias_hbm,
    ids_hbm,
    count_hbm,
    upstream_hbm,
    weight_out,
    tile_out,
    fine,
    selector,
    conv_w,
    query_w,
    out_w,
    kv,
    bias_in,
    ids_in,
    count_in,
    upstream,
    meta,
    halo,
    t_even,
    t_odd,
    pre,
    feat,
    query,
    grad_att,
    grad_query,
    acc,
    metas,
    kv_send,
    kv_recv,
    slot_send,
    slot_recv,
    picks,
    rep_send,
    rep_recv,
    sub_send,
    sub_recv,
    part,
    dp_send,
    dp_recv,
    load_sem,
    halo_sem,
    meta_sem,
    kv_sem,
    slot_sem,
    rep_sem,
    sub_sem,
    dp_sem,
):
    dps, subs, tiles, cap, slots, rows_dev, reduce_here = cfg
    me = lax.axis_index("dp")
    sub = lax.axis_index("sub")
    rep = lax.axis_index("rep")
    cap_rows = cap * 16
    planes = t_even.shape[0]
    cells = t_even.shape[1]
    channels = fine.shape[2]
    lanes = slots * 8
    pairs = query.shape[1] // 128
    place_rows = dps * cap_rows
    peers = [lax.rem(me + d, dps) for d in range(dps)]

    barrier = pltpu.get_barrier_semaphore()
    greeted = 0
    for d in range(1, dps):
        pl.semaphore_signal(barrier, inc=1, device_id={"dp": peers[d]}, device_id_type=MESH)
        greeted += 1
    for step in (1, subs - 1) if subs > 2 else (1,):
        pl.semaphore_signal(
            barrier, inc=1, device_id={"sub": lax.rem(sub + step, subs)}, device_id_type=MESH
        )
        greeted += 1
    pl.semaphore_signal(barrier, inc=1, device_id={"rep": 1 - rep}, device_id_type=MESH)
    greeted += 1

    loads = []
    for i, (src, dst) in enumerate(
        (
            (ids_hbm, ids_in),
            (bias_hbm, bias_in),
            (count_hbm, count_in),
            (selector_hbm, selector),
            (fine_hbm, fine),
            (kv_hbm, kv),
            (upstream_hbm, upstream),
            (out_w_hbm, out_w),
            (conv_w_hbm, conv_w),
            (query_w_hbm, query_w),
        )
    ):
        copy = pltpu.make_async_copy(src, dst, load_sem.at[i])
        copy.start()
        loads.append(copy)

    def send(src, dst, sems, index, where):
        return pltpu.make_async_remote_copy(
            src_ref=src,
            dst_ref=dst,
            send_sem=sems.at[0, index],
            recv_sem=sems.at[1, index],
            device_id=where,
            device_id_type=MESH,
        )

    for i in range(3):
        loads[i].wait()
    spread = jnp.where(iota((slots, lanes), 0) == iota((slots, lanes), 1) // 8, 1.0, 0.0)
    ids_row = dot(ids_in[...].astype(BF16), spread.astype(BF16))
    key_of = jnp.where(iota((8, lanes), 0) == iota((8, lanes), 1) % 8, 1.0, 0.0)
    meta[:tiles, :] = dot_tn(bias_in[...], key_of.astype(BF16))
    meta[tiles:, :] = jnp.broadcast_to(ids_row, (8, lanes))
    metas[me] = meta[...]
    count = count_in[...].astype(F32)

    pl.semaphore_wait(barrier, greeted)
    meta_copies = [
        send(meta, metas.at[me], meta_sem, d, {"dp": peers[d]}) for d in range(1, dps)
    ]
    for copy in meta_copies:
        copy.start()
    loads[3].wait()
    loads[4].wait()
    halo_copy = send(
        fine.at[2 * planes - 1], halo, halo_sem, 0, {"sub": lax.rem(sub + 1, subs)}
    )
    halo_copy.start()

    def spread_taps(found, target, index):
        for tap in range(9):
            target[index, :, tap * channels : (tap + 1) * channels] = found[
                tap * cells : (tap + 1) * cells
            ]

    def unfold(i, carry):
        pair = jnp.concatenate([fine[2 * i], fine[2 * i + 1]], axis=1)
        found = dot(selector[...], pair).astype(BF16)
        spread_taps(found[:, :channels], t_even, i)
        spread_taps(found[:, channels:], t_odd, i + 1)
        return carry

    early = planes // 2
    lax.fori_loop(0, early, unfold, 0)

    def slot_dest(ids_row):
        owner_row = jnp.floor(ids_row * (1.0 / tiles))
        owner_col = jnp.transpose(jnp.broadcast_to(owner_row, (lanes, lanes)))
        earlier = (iota((lanes, lanes), 0) // 8) < (iota((lanes, lanes), 1) // 8)
        same = jnp.where((owner_col == owner_row) & earlier, 1.0, 0.0)
        rank = jnp.sum(same, axis=0, keepdims=True) * 0.125
        return owner_row * cap + rank

    me_f = me.astype(F32)

    def picker(ids_row):
        dest = slot_dest(ids_row)
        slot_row = (iota((cap_rows, lanes), 0) // 16).astype(F32) + me_f * cap
        first = (iota((cap_rows, lanes), 1) % 8) == 0
        by_slot = jnp.where((slot_row == dest) & first, 1.0, 0.0).astype(BF16)
        tile_row = (iota((tiles * 16, lanes), 0) // 16).astype(F32) + me_f * tiles
        by_tile = jnp.where(tile_row == ids_row, 1.0, 0.0).astype(BF16)
        matched = dot_nt(by_slot, by_tile)
        unit = (iota(matched.shape, 0) % 16) == (iota(matched.shape, 1) % 16)
        return jnp.where(unit, matched, 0.0).astype(BF16)

    for copy in meta_copies:
        copy.wait()
    loads[5].wait()
    for p in range(dps):
        picks[p] = picker(metas[p, tiles : tiles + 1, :])
    kv_copies = []
    for j in range(pairs):
        cut = slice(j * 128, (j + 1) * 128)
        chosen = dot(picks[...].reshape(place_rows, tiles * 16), kv[:, cut]).astype(BF16)
        kv_send[j] = chosen.reshape(dps, cap_rows, 128)
        group = []
        for d in range(dps - 1, 0, -1):
            copy = send(
                kv_send.at[j, peers[d]],
                kv_recv.at[j, me],
                kv_sem,
                j * dps + d,
                {"dp": peers[d]},
            )
            copy.start()
            group.append(copy)
        kv_copies.append(group)
        kv_recv[j, me] = kv_send[j, me]

    lax.fori_loop(early, planes, unfold, 0)
    halo_copy.wait()
    edge = dot(selector[...], halo[...])
    edge = jnp.where(sub > 0, edge, 0.0).astype(BF16)
    spread_taps(edge, t_odd, 0)

    row_count = planes * cells

    def columns(a):
        if a == 1:
            return t_even[...].reshape(row_count, 9 * channels)
        start = a // 2
        return t_odd[start : start + planes].reshape(row_count, 9 * channels)

    for i in range(6, 10):
        loads[i].wait()
    value = dot(columns(0), conv_w[0]) + dot(columns(1), conv_w[1]) + dot(columns(2), conv_w[2])
    pre[...] = value
    feat[...] = (value * jax.nn.sigmoid(value)).astype(BF16)
    query[...] = dot(feat[...], query_w[...]).astype(BF16)
    grad_att[...] = dot_nt(upstream[...], out_w[...]).astype(BF16)

    ids_row = meta[tiles : tiles + 1, :]
    dest = slot_dest(ids_row)
    dest2 = jnp.concatenate([dest, dest], axis=1)
    row_i = iota((place_rows, 2 * lanes), 0)
    lane_i = iota((place_rows, 2 * lanes), 1)
    fits = ((row_i // 16).astype(F32) == dest2) & (
        (row_i % 16) == (lane_i // lanes) * 8 + lane_i % 8
    )
    placing = jnp.where(fits, 1.0, 0.0).astype(BF16)

    bias = jnp.zeros((1, lanes), F32)
    for owner in range(dps):
        tile_row = iota((tiles, lanes), 0).astype(F32) + float(owner * tiles)
        bias = bias + jnp.sum(
            jnp.where(tile_row == ids_row, metas[owner, :tiles, :], 0.0), axis=0, keepdims=True
        )
    lane_slot = (iota((1, lanes), 1) // 8).astype(F32)
    bias = jnp.where(lane_slot < count, bias, -jnp.inf)

    low = iota((lanes, 128), 1) < 64
    conv_rows = 27 * channels
    out_rows = conv_rows + pairs * channels
    slot_copies = []
    for j in range(pairs):
        for copy in kv_copies[j]:
            copy.wait()
        kv_pair = dot_tn(placing, kv_recv[j].reshape(place_rows, 128)).astype(BF16)
        cut = slice(j * 128, (j + 1) * 128)
        keys = kv_pair[:lanes]
        values = kv_pair[lanes:]
        none = jnp.zeros_like(keys)
        keys2 = jnp.concatenate(
            [jnp.where(low, keys, none), jnp.where(low, none, keys)], axis=0
        )
        values2 = jnp.concatenate(
            [jnp.where(low, values, none), jnp.where(low, none, values)], axis=0
        )
        q = query[:, cut]
        g = grad_att[:, cut]
        scores = dot_nt(q, keys2) * 0.125
        grad_prob = dot_nt(g, values2)
        probs = []
        gs = []
        for h in range(2):
            s = scores[:, h * lanes : (h + 1) * lanes] + bias
            e = jnp.exp(s - jnp.max(s, axis=1, keepdims=True))
            prob = e * (1.0 / jnp.sum(e, axis=1, keepdims=True))
            gp = grad_prob[:, h * lanes : (h + 1) * lanes]
            probs.append(prob.astype(BF16))
            gs.append((prob * (gp - jnp.sum(prob * gp, axis=1, keepdims=True))).astype(BF16))
        prob_b = jnp.concatenate(probs, axis=1)
        grad_s = jnp.concatenate(gs, axis=1)
        gv = dot_tn(prob_b, g)
        gk = dot_tn(grad_s, q) * 0.125
        grad_pair = jnp.concatenate(
            [
                jnp.where(low, gk[:lanes], gk[lanes:]).astype(BF16),
                jnp.where(low, gv[:lanes], gv[lanes:]).astype(BF16),
            ],
            axis=0,
        )
        slot_send[j] = dot(placing, grad_pair).astype(BF16).reshape(dps, cap_rows, 128)
        group = []
        for d in range(dps - 1, 0, -1):
            copy = send(
                slot_send.at[j, peers[d]],
                slot_recv.at[j, me],
                slot_sem,
                j * dps + d,
                {"dp": peers[d]},
            )
            copy.start()
            group.append(copy)
        slot_copies.append(group)
        slot_recv[j, me] = slot_send[j, me]
        attended = dot(prob_b, values2).astype(BF16)
        acc[out_rows + j * 128 : out_rows + (j + 1) * 128, :] = dot_tn(attended, upstream[...])
        gq = (dot(grad_s, keys2) * 0.125).astype(BF16)
        grad_query[:, cut] = gq
        acc[pl.ds(conv_rows + j, channels, stride=pairs), :] = dot_tn(feat[...], gq)

    grad_feat = upstream[...].astype(F32) + dot_nt(grad_query[...], query_w[...])
    v = pre[...]
    sig = jax.nn.sigmoid(v)
    grad_pre = (grad_feat * (sig * (1.0 + v * (1.0 - sig)))).astype(BF16)

    def conv_grad(a):
        acc[a * 9 * channels : (a + 1) * 9 * channels, :] = dot_tn(columns(a), grad_pre)

    def scatter_tiles(j):
        for copy in slot_copies[j]:
            copy.wait()
        tile_out[:, j * 128 : (j + 1) * 128] = dot_tn(
            picks[...].reshape(place_rows, tiles * 16), slot_recv[j].reshape(place_rows, 128)
        )

    if not reduce_here:
        for a in range(3):
            conv_grad(a)
        for j in range(pairs):
            scatter_tiles(j)
        weight_out[...] = acc[: weight_out.shape[0], :]
        return

    pad_rows = rep_send.shape[2]
    acc[acc.shape[0] - 8 :, :] = jnp.zeros((8, 128), F32)

    def chunk(p, s, r):
        start = pl.multiple_of(((p * subs + s) * 2 + r) * rows_dev, 8)
        return acc[pl.ds(start, pad_rows), :]

    rep_copies = [
        send(rep_send.at[p], rep_recv.at[p], rep_sem, p, {"rep": 1 - rep}) for p in range(dps)
    ]
    sub_copies = [
        send(sub_send.at[p], sub_recv.at[p], sub_sem, p, {"sub": 1 - sub}) for p in range(dps)
    ]

    def start_rep(p):
        rep_send[p, 0] = chunk(p, 1 - sub, 1 - rep).astype(BF16)
        rep_send[p, 1] = chunk(p, sub, 1 - rep).astype(BF16)
        rep_copies[p].start()

    def start_sub(p):
        rep_copies[p].wait()
        sub_send[p] = (chunk(p, 1 - sub, rep) + rep_recv[p, 0].astype(F32)).astype(BF16)
        sub_copies[p].start()
        part[p] = chunk(p, sub, rep) + rep_recv[p, 1].astype(F32)

    def start_dp(p):
        sub_copies[p].wait()
        part[p] = part[p] + sub_recv[p].astype(F32)

        @pl.when(me != p)
        def _():
            dp_send[p] = part[p].astype(BF16)
            d = lax.rem(p - me + dps, dps)
            send(dp_send.at[p], dp_recv.at[d], dp_sem, d, {"dp": p}).start()

    done_rep = done_sub = 0
    for a in range(3):
        conv_grad(a)
        ready = dps if a == 2 else (a + 1) * 9 * channels // (4 * rows_dev)
        if a > 0 and done_sub < done_rep:
            start_sub(done_sub)
            done_sub += 1
        while done_rep < ready:
            start_rep(done_rep)
            done_rep += 1
    for p in range(dps):
        if done_sub < dps:
            start_sub(done_sub)
            done_sub += 1
        start_dp(p)
    for j in range(pairs):
        scatter_tiles(j)
    total = part[me]
    for d in range(1, dps):
        send(dp_send.at[peers[d]], dp_recv.at[d], dp_sem, d, {"dp": peers[d]}).wait()
        total = total + dp_recv[d].astype(F32)
    weight_out[...] = total[:rows_dev]


def per_device(
    fine,
    conv_weight,
    query_weight,
    out_weight,
    coarse_kv,
    key_bias,
    zone_ids,
    zone_counts,
    grad_out,
):
    strip_len, side, _, channels = fine.shape[1:]
    inner = query_weight.shape[1]
    tiles = coarse_kv.shape[1]
    slots = zone_ids.shape[1] * zone_ids.shape[2]
    dps, subs, reps = lax.axis_size("dp"), lax.axis_size("sub"), lax.axis_size("rep")
    cap = 2 * slots // dps
    cap_rows = cap * 16
    lanes = slots * 8
    planes = strip_len // 2
    cells = (side // 2) ** 2
    rows = planes * cells
    weight_rows = (27 * channels * channels + 2 * channels * inner) // 128
    devices = dps * subs * reps
    reduce_here = subs == 2 and weight_rows % (8 * devices) == 0
    rows_dev = weight_rows // devices if reduce_here else 16
    pad_rows = -(-rows_dev // 16) * 16
    cfg = (dps, subs, tiles, cap, slots, rows_dev, reduce_here)
    weight_shape = (rows_dev, 128) if reduce_here else (weight_rows, 128)
    vmem = pl.BlockSpec(memory_space=pltpu.VMEM)
    pairs = inner // 128
    hbm = pl.BlockSpec(memory_space=pltpu.HBM)
    weight_out, tile_out = pl.pallas_call(
        functools.partial(kernel, cfg),
        out_shape=(
            jax.ShapeDtypeStruct(weight_shape, F32),
            jax.ShapeDtypeStruct((tiles * 16, inner), F32),
        ),
        in_specs=[hbm] * 10,
        out_specs=(vmem, vmem),
        scratch_shapes=[
            pltpu.VMEM((strip_len, side * side, channels), BF16),
            pltpu.VMEM((9 * cells, side * side), BF16),
            pltpu.VMEM((3, 9 * channels, channels), BF16),
            pltpu.VMEM((channels, inner), BF16),
            pltpu.VMEM((inner, channels), BF16),
            pltpu.VMEM((tiles * 16, inner), BF16),
            pltpu.VMEM((8, tiles), BF16),
            pltpu.VMEM((1, slots), jnp.int32),
            pltpu.VMEM((1, 1), jnp.int32),
            pltpu.VMEM((rows, channels), BF16),
            pltpu.VMEM((tiles + 8, lanes), F32),
            pltpu.VMEM((side * side, channels), BF16),
            pltpu.VMEM((planes, cells, 9 * channels), BF16),
            pltpu.VMEM((planes + 1, cells, 9 * channels), BF16),
            pltpu.VMEM((rows, channels), F32),
            pltpu.VMEM((rows, channels), BF16),
            pltpu.VMEM((rows, inner), BF16),
            pltpu.VMEM((rows, inner), BF16),
            pltpu.VMEM((rows, inner), BF16),
            pltpu.VMEM((weight_rows + 8, 128), F32),
            pltpu.VMEM((dps, tiles + 8, lanes), F32),
            pltpu.VMEM((pairs, dps, cap_rows, 128), BF16),
            pltpu.VMEM((pairs, dps, cap_rows, 128), BF16),
            pltpu.VMEM((pairs, dps, cap_rows, 128), BF16),
            pltpu.VMEM((pairs, dps, cap_rows, 128), BF16),
            pltpu.VMEM((dps, cap_rows, tiles * 16), BF16),
            pltpu.VMEM((dps, 2, pad_rows, 128), BF16),
            pltpu.VMEM((dps, 2, pad_rows, 128), BF16),
            pltpu.VMEM((dps, pad_rows, 128), BF16),
            pltpu.VMEM((dps, pad_rows, 128), BF16),
            pltpu.VMEM((dps, pad_rows, 128), F32),
            pltpu.VMEM((dps, pad_rows, 128), BF16),
            pltpu.VMEM((dps, pad_rows, 128), BF16),
            pltpu.SemaphoreType.DMA((10,)),
            pltpu.SemaphoreType.DMA((2, 1)),
            pltpu.SemaphoreType.DMA((2, dps)),
            pltpu.SemaphoreType.DMA((2, pairs * dps)),
            pltpu.SemaphoreType.DMA((2, pairs * dps)),
            pltpu.SemaphoreType.DMA((2, dps)),
            pltpu.SemaphoreType.DMA((2, dps)),
            pltpu.SemaphoreType.DMA((2, dps)),
        ],
        compiler_params=pltpu.CompilerParams(
            collective_id=0, has_side_effects=True, vmem_limit_bytes=64 * 1024 * 1024 - 256 * 1024
        ),
    )(
        fine[0].reshape(strip_len, side * side, channels),
        jnp.asarray(tap_selector(side), BF16),
        conv_weight.reshape(3, 9 * channels, channels),
        query_weight,
        out_weight,
        coarse_kv[0].reshape(tiles * 16, inner),
        key_bias[0].T,
        zone_ids[0].reshape(1, slots),
        zone_counts[:, :1],
        grad_out[0].reshape(rows, channels),
    )
    weight_grads = weight_out.reshape(-1)
    if not reduce_here:
        weight_grads = lax.psum_scatter(
            weight_grads, ("dp", "sub", "rep"), scatter_dimension=0, tiled=True
        )
    return (weight_grads, tile_out.reshape(1, tiles, 2, 8, inner))


def solution(mesh):
    in_specs = (
        P(("grp", "dp", "rep"), "sub", None, None, None),
        P(),
        P(),
        P(),
        P(("grp", "sub", "rep"), "dp", None, None, None),
        P(("grp", "sub", "rep"), "dp", None),
        P(("grp", "dp", "rep"), "sub", None),
        P(("grp", "dp", "rep"), "sub"),
        P(("grp", "dp", "rep"), "sub", None, None, None),
    )
    out_specs = (P(("grp", "dp", "sub", "rep")), P(("grp", "sub", "rep"), "dp", None, None, None))
    return jax.shard_map(
        per_device, mesh=mesh, in_specs=in_specs, out_specs=out_specs, check_vma=False
    )
```

```python
import functools

import jax
import jax.numpy as jnp
import numpy as np
from jax import lax
from jax.experimental import pallas as pl
from jax.experimental.pallas import tpu as pltpu
from jax.sharding import PartitionSpec as P

HEADS = 8
MESH = pl.DeviceIdType.MESH
F32 = jnp.float32
BF16 = jnp.bfloat16


def dot(a, b):
    return jnp.dot(a, b, preferred_element_type=F32)


def dot_nt(a, b):
    return lax.dot_general(a, b, (((1,), (1,)), ((), ())), preferred_element_type=F32)


def dot_tn(a, b):
    return lax.dot_general(a, b, (((0,), (0,)), ((), ())), preferred_element_type=F32)


def iota(shape, dim):
    return lax.broadcasted_iota(jnp.int32, shape, dim)


def tap_selector(side):
    half = side // 2
    sel = np.zeros((9, half, half, side, side), np.float32)
    for b in range(3):
        for c in range(3):
            for y in range(half):
                for z in range(half):
                    yy, zz = 2 * y + b - 1, 2 * z + c - 1
                    if yy >= 0 and zz >= 0:
                        sel[b * 3 + c, y, z, yy, zz] = 1.0
    return sel.reshape(9 * half * half, side * side)


def kernel(
    cfg,
    fine_hbm,
    selector_hbm,
    conv_w_hbm,
    query_w_hbm,
    out_w_hbm,
    kv_hbm,
    bias_hbm,
    ids_hbm,
    count_hbm,
    upstream_hbm,
    weight_out,
    tile_out,
    fine,
    selector,
    conv_w,
    query_w,
    out_w,
    kv,
    bias_in,
    ids_in,
    count_in,
    upstream,
    meta,
    halo,
    t_even,
    t_odd,
    pre,
    feat,
    query,
    grad_att,
    grad_query,
    acc,
    metas,
    kv_send,
    kv_recv,
    slot_send,
    slot_recv,
    picks,
    rep_send,
    rep_recv,
    sub_send,
    sub_recv,
    part,
    dp_send,
    dp_recv,
    load_sem,
    halo_sem,
    meta_sem,
    kv_sem,
    slot_sem,
    rep_sem,
    sub_sem,
    dp_sem,
):
    dps, subs, tiles, cap, slots, rows_dev, reduce_here = cfg
    me = lax.axis_index("dp")
    sub = lax.axis_index("sub")
    rep = lax.axis_index("rep")
    cap_rows = cap * 16
    planes = t_even.shape[0]
    cells = t_even.shape[1]
    channels = fine.shape[2]
    lanes = slots * 8
    pairs = query.shape[1] // 128
    place_rows = dps * cap_rows
    peers = [lax.rem(me + d, dps) for d in range(dps)]

    barrier = pltpu.get_barrier_semaphore()
    greeted = 0
    for d in range(1, dps):
        pl.semaphore_signal(barrier, inc=1, device_id={"dp": peers[d]}, device_id_type=MESH)
        greeted += 1
    for step in (1, subs - 1) if subs > 2 else (1,):
        pl.semaphore_signal(
            barrier, inc=1, device_id={"sub": lax.rem(sub + step, subs)}, device_id_type=MESH
        )
        greeted += 1
    pl.semaphore_signal(barrier, inc=1, device_id={"rep": 1 - rep}, device_id_type=MESH)
    greeted += 1

    loads = []
    for i, (src, dst) in enumerate(
        (
            (ids_hbm, ids_in),
            (bias_hbm, bias_in),
            (count_hbm, count_in),
            (selector_hbm, selector),
            (fine_hbm, fine),
            (kv_hbm, kv),
            (upstream_hbm, upstream),
            (out_w_hbm, out_w),
            (conv_w_hbm, conv_w),
            (query_w_hbm, query_w),
        )
    ):
        copy = pltpu.make_async_copy(src, dst, load_sem.at[i])
        copy.start()
        loads.append(copy)

    def send(src, dst, sems, index, where):
        return pltpu.make_async_remote_copy(
            src_ref=src,
            dst_ref=dst,
            send_sem=sems.at[0, index],
            recv_sem=sems.at[1, index],
            device_id=where,
            device_id_type=MESH,
        )

    for i in range(3):
        loads[i].wait()
    spread = jnp.where(iota((slots, lanes), 0) == iota((slots, lanes), 1) // 8, 1.0, 0.0)
    ids_row = dot(ids_in[...].astype(BF16), spread.astype(BF16))
    key_of = jnp.where(iota((8, lanes), 0) == iota((8, lanes), 1) % 8, 1.0, 0.0)
    meta[:tiles, :] = dot_tn(bias_in[...], key_of.astype(BF16))
    meta[tiles:, :] = jnp.broadcast_to(ids_row, (8, lanes))
    metas[me] = meta[...]
    count = count_in[...].astype(F32)

    pl.semaphore_wait(barrier, greeted)
    meta_copies = [
        send(meta, metas.at[me], meta_sem, d, {"dp": peers[d]}) for d in range(1, dps)
    ]
    for copy in meta_copies:
        copy.start()
    loads[3].wait()
    loads[4].wait()
    halo_copy = send(
        fine.at[2 * planes - 1], halo, halo_sem, 0, {"sub": lax.rem(sub + 1, subs)}
    )
    halo_copy.start()

    def spread_taps(found, target, index):
        for tap in range(9):
            target[index, :, tap * channels : (tap + 1) * channels] = found[
                tap * cells : (tap + 1) * cells
            ]

    def unfold(i, carry):
        pair = jnp.concatenate([fine[2 * i], fine[2 * i + 1]], axis=1)
        found = dot(selector[...], pair).astype(BF16)
        spread_taps(found[:, :channels], t_even, i)
        spread_taps(found[:, channels:], t_odd, i + 1)
        return carry

    early = planes // 2
    lax.fori_loop(0, early, unfold, 0)

    def slot_dest(ids_row):
        owner_row = jnp.floor(ids_row * (1.0 / tiles))
        owner_col = jnp.transpose(jnp.broadcast_to(owner_row, (lanes, lanes)))
        earlier = (iota((lanes, lanes), 0) // 8) < (iota((lanes, lanes), 1) // 8)
        same = jnp.where((owner_col == owner_row) & earlier, 1.0, 0.0)
        rank = jnp.sum(same, axis=0, keepdims=True) * 0.125
        return owner_row * cap + rank

    me_f = me.astype(F32)

    def picker(ids_row):
        dest = slot_dest(ids_row)
        slot_row = (iota((cap_rows, lanes), 0) // 16).astype(F32) + me_f * cap
        first = (iota((cap_rows, lanes), 1) % 8) == 0
        by_slot = jnp.where((slot_row == dest) & first, 1.0, 0.0).astype(BF16)
        tile_row = (iota((tiles * 16, lanes), 0) // 16).astype(F32) + me_f * tiles
        by_tile = jnp.where(tile_row == ids_row, 1.0, 0.0).astype(BF16)
        matched = dot_nt(by_slot, by_tile)
        unit = (iota(matched.shape, 0) % 16) == (iota(matched.shape, 1) % 16)
        return jnp.where(unit, matched, 0.0).astype(BF16)

    for copy in meta_copies:
        copy.wait()
    loads[5].wait()
    for p in range(dps):
        picks[p] = picker(metas[p, tiles : tiles + 1, :])
    kv_copies = []
    for j in range(pairs):
        cut = slice(j * 128, (j + 1) * 128)
        chosen = dot(picks[...].reshape(place_rows, tiles * 16), kv[:, cut]).astype(BF16)
        kv_send[j] = chosen.reshape(dps, cap_rows, 128)
        group = []
        for d in range(dps - 1, 0, -1):
            copy = send(
                kv_send.at[j, peers[d]],
                kv_recv.at[j, me],
                kv_sem,
                j * dps + d,
                {"dp": peers[d]},
            )
            copy.start()
            group.append(copy)
        kv_copies.append(group)
        kv_recv[j, me] = kv_send[j, me]

    lax.fori_loop(early, planes, unfold, 0)
    halo_copy.wait()
    edge = dot(selector[...], halo[...])
    edge = jnp.where(sub > 0, edge, 0.0).astype(BF16)
    spread_taps(edge, t_odd, 0)

    row_count = planes * cells

    def columns(a):
        if a == 1:
            return t_even[...].reshape(row_count, 9 * channels)
        start = a // 2
        return t_odd[start : start + planes].reshape(row_count, 9 * channels)

    for i in range(6, 10):
        loads[i].wait()
    value = dot(columns(0), conv_w[0]) + dot(columns(1), conv_w[1]) + dot(columns(2), conv_w[2])
    pre[...] = value
    feat[...] = (value * jax.nn.sigmoid(value)).astype(BF16)
    query[...] = dot(feat[...], query_w[...]).astype(BF16)
    grad_att[...] = dot_nt(upstream[...], out_w[...]).astype(BF16)

    ids_row = meta[tiles : tiles + 1, :]
    dest = slot_dest(ids_row)
    dest2 = jnp.concatenate([dest, dest], axis=1)
    row_i = iota((place_rows, 2 * lanes), 0)
    lane_i = iota((place_rows, 2 * lanes), 1)
    fits = ((row_i // 16).astype(F32) == dest2) & (
        (row_i % 16) == (lane_i // lanes) * 8 + lane_i % 8
    )
    placing = jnp.where(fits, 1.0, 0.0).astype(BF16)

    bias = jnp.zeros((1, lanes), F32)
    for owner in range(dps):
        tile_row = iota((tiles, lanes), 0).astype(F32) + float(owner * tiles)
        bias = bias + jnp.sum(
            jnp.where(tile_row == ids_row, metas[owner, :tiles, :], 0.0), axis=0, keepdims=True
        )
    lane_slot = (iota((1, lanes), 1) // 8).astype(F32)
    bias = jnp.where(lane_slot < count, bias, -jnp.inf)

    low = iota((lanes, 128), 1) < 64
    conv_rows = 27 * channels
    out_rows = conv_rows + pairs * channels
    slot_copies = []

    def start_slots(j):
        group = []
        for d in range(dps - 1, 0, -1):
            copy = send(
                slot_send.at[j, peers[d]],
                slot_recv.at[j, me],
                slot_sem,
                j * dps + d,
                {"dp": peers[d]},
            )
            copy.start()
            group.append(copy)
        slot_copies.append(group)

    for j in range(pairs):
        for copy in kv_copies[j]:
            copy.wait()
        if j == pairs - 1:
            for i in range(pairs - 1):
                start_slots(i)
        kv_pair = dot_tn(placing, kv_recv[j].reshape(place_rows, 128)).astype(BF16)
        cut = slice(j * 128, (j + 1) * 128)
        keys = kv_pair[:lanes]
        values = kv_pair[lanes:]
        none = jnp.zeros_like(keys)
        keys2 = jnp.concatenate(
            [jnp.where(low, keys, none), jnp.where(low, none, keys)], axis=0
        )
        values2 = jnp.concatenate(
            [jnp.where(low, values, none), jnp.where(low, none, values)], axis=0
        )
        q = query[:, cut]
        g = grad_att[:, cut]
        scores = dot_nt(q, keys2) * 0.125
        grad_prob = dot_nt(g, values2)
        probs = []
        gs = []
        for h in range(2):
            s = scores[:, h * lanes : (h + 1) * lanes] + bias
            e = jnp.exp(s - jnp.max(s, axis=1, keepdims=True))
            prob = e * (1.0 / jnp.sum(e, axis=1, keepdims=True))
            gp = grad_prob[:, h * lanes : (h + 1) * lanes]
            probs.append(prob.astype(BF16))
            gs.append((prob * (gp - jnp.sum(prob * gp, axis=1, keepdims=True))).astype(BF16))
        prob_b = jnp.concatenate(probs, axis=1)
        grad_s = jnp.concatenate(gs, axis=1)
        gv = dot_tn(prob_b, g)
        gk = dot_tn(grad_s, q) * 0.125
        grad_pair = jnp.concatenate(
            [
                jnp.where(low, gk[:lanes], gk[lanes:]).astype(BF16),
                jnp.where(low, gv[:lanes], gv[lanes:]).astype(BF16),
            ],
            axis=0,
        )
        slot_send[j] = dot(placing, grad_pair).astype(BF16).reshape(dps, cap_rows, 128)
        if j == pairs - 1:
            start_slots(j)
        slot_recv[j, me] = slot_send[j, me]
        attended = dot(prob_b, values2).astype(BF16)
        acc[out_rows + j * 128 : out_rows + (j + 1) * 128, :] = dot_tn(attended, upstream[...])
        gq = (dot(grad_s, keys2) * 0.125).astype(BF16)
        grad_query[:, cut] = gq
        acc[pl.ds(conv_rows + j, channels, stride=pairs), :] = dot_tn(feat[...], gq)

    grad_feat = upstream[...].astype(F32) + dot_nt(grad_query[...], query_w[...])
    v = pre[...]
    sig = jax.nn.sigmoid(v)
    grad_pre = (grad_feat * (sig * (1.0 + v * (1.0 - sig)))).astype(BF16)

    def conv_grad(a):
        acc[a * 9 * channels : (a + 1) * 9 * channels, :] = dot_tn(columns(a), grad_pre)

    def scatter_tiles(j):
        for copy in slot_copies[j]:
            copy.wait()
        tile_out[:, j * 128 : (j + 1) * 128] = dot_tn(
            picks[...].reshape(place_rows, tiles * 16), slot_recv[j].reshape(place_rows, 128)
        )

    if not reduce_here:
        for a in range(3):
            conv_grad(a)
        for j in range(pairs):
            scatter_tiles(j)
        weight_out[...] = acc[: weight_out.shape[0], :]
        return

    pad_rows = rep_send.shape[2]
    acc[acc.shape[0] - 8 :, :] = jnp.zeros((8, 128), F32)

    def chunk(p, s, r):
        start = pl.multiple_of(((p * subs + s) * 2 + r) * rows_dev, 8)
        return acc[pl.ds(start, pad_rows), :]

    rep_copies = [
        send(rep_send.at[p], rep_recv.at[p], rep_sem, p, {"rep": 1 - rep}) for p in range(dps)
    ]
    sub_copies = [
        send(sub_send.at[p], sub_recv.at[p], sub_sem, p, {"sub": 1 - sub}) for p in range(dps)
    ]

    def start_rep(p):
        rep_send[p, 0] = chunk(p, 1 - sub, 1 - rep).astype(BF16)
        rep_send[p, 1] = chunk(p, sub, 1 - rep).astype(BF16)
        rep_copies[p].start()

    def start_sub(p):
        rep_copies[p].wait()
        sub_send[p] = (chunk(p, 1 - sub, rep) + rep_recv[p, 0].astype(F32)).astype(BF16)
        sub_copies[p].start()
        part[p] = chunk(p, sub, rep) + rep_recv[p, 1].astype(F32)

    def start_dp(p):
        sub_copies[p].wait()
        part[p] = part[p] + sub_recv[p].astype(F32)

        @pl.when(me != p)
        def _():
            dp_send[p] = part[p].astype(BF16)
            d = lax.rem(p - me + dps, dps)
            send(dp_send.at[p], dp_recv.at[d], dp_sem, d, {"dp": p}).start()

    done_rep = done_sub = 0
    for a in range(3):
        conv_grad(a)
        ready = dps if a == 2 else (a + 1) * 9 * channels // (4 * rows_dev)
        if a > 0 and done_sub < done_rep:
            start_sub(done_sub)
            done_sub += 1
        while done_rep < ready:
            start_rep(done_rep)
            done_rep += 1
    late = list(range(done_sub, dps))[::-1]
    for p in late:
        start_sub(p)
    for p in list(range(done_sub)) + late:
        start_dp(p)
    for j in range(pairs):
        scatter_tiles(j)
    total = part[me]
    for d in range(1, dps):
        send(dp_send.at[peers[d]], dp_recv.at[d], dp_sem, d, {"dp": peers[d]}).wait()
        total = total + dp_recv[d].astype(F32)
    weight_out[...] = total[:rows_dev]


def per_device(
    fine,
    conv_weight,
    query_weight,
    out_weight,
    coarse_kv,
    key_bias,
    zone_ids,
    zone_counts,
    grad_out,
):
    strip_len, side, _, channels = fine.shape[1:]
    inner = query_weight.shape[1]
    tiles = coarse_kv.shape[1]
    slots = zone_ids.shape[1] * zone_ids.shape[2]
    dps, subs, reps = lax.axis_size("dp"), lax.axis_size("sub"), lax.axis_size("rep")
    cap = 2 * slots // dps
    cap_rows = cap * 16
    lanes = slots * 8
    planes = strip_len // 2
    cells = (side // 2) ** 2
    rows = planes * cells
    weight_rows = (27 * channels * channels + 2 * channels * inner) // 128
    devices = dps * subs * reps
    reduce_here = subs == 2 and weight_rows % (8 * devices) == 0
    rows_dev = weight_rows // devices if reduce_here else 16
    pad_rows = -(-rows_dev // 16) * 16
    cfg = (dps, subs, tiles, cap, slots, rows_dev, reduce_here)
    weight_shape = (rows_dev, 128) if reduce_here else (weight_rows, 128)
    vmem = pl.BlockSpec(memory_space=pltpu.VMEM)
    pairs = inner // 128
    hbm = pl.BlockSpec(memory_space=pltpu.HBM)
    weight_out, tile_out = pl.pallas_call(
        functools.partial(kernel, cfg),
        out_shape=(
            jax.ShapeDtypeStruct(weight_shape, F32),
            jax.ShapeDtypeStruct((tiles * 16, inner), F32),
        ),
        in_specs=[hbm] * 10,
        out_specs=(vmem, vmem),
        scratch_shapes=[
            pltpu.VMEM((strip_len, side * side, channels), BF16),
            pltpu.VMEM((9 * cells, side * side), BF16),
            pltpu.VMEM((3, 9 * channels, channels), BF16),
            pltpu.VMEM((channels, inner), BF16),
            pltpu.VMEM((inner, channels), BF16),
            pltpu.VMEM((tiles * 16, inner), BF16),
            pltpu.VMEM((8, tiles), BF16),
            pltpu.VMEM((1, slots), jnp.int32),
            pltpu.VMEM((1, 1), jnp.int32),
            pltpu.VMEM((rows, channels), BF16),
            pltpu.VMEM((tiles + 8, lanes), F32),
            pltpu.VMEM((side * side, channels), BF16),
            pltpu.VMEM((planes, cells, 9 * channels), BF16),
            pltpu.VMEM((planes + 1, cells, 9 * channels), BF16),
            pltpu.VMEM((rows, channels), F32),
            pltpu.VMEM((rows, channels), BF16),
            pltpu.VMEM((rows, inner), BF16),
            pltpu.VMEM((rows, inner), BF16),
            pltpu.VMEM((rows, inner), BF16),
            pltpu.VMEM((weight_rows + 8, 128), F32),
            pltpu.VMEM((dps, tiles + 8, lanes), F32),
            pltpu.VMEM((pairs, dps, cap_rows, 128), BF16),
            pltpu.VMEM((pairs, dps, cap_rows, 128), BF16),
            pltpu.VMEM((pairs, dps, cap_rows, 128), BF16),
            pltpu.VMEM((pairs, dps, cap_rows, 128), BF16),
            pltpu.VMEM((dps, cap_rows, tiles * 16), BF16),
            pltpu.VMEM((dps, 2, pad_rows, 128), BF16),
            pltpu.VMEM((dps, 2, pad_rows, 128), BF16),
            pltpu.VMEM((dps, pad_rows, 128), BF16),
            pltpu.VMEM((dps, pad_rows, 128), BF16),
            pltpu.VMEM((dps, pad_rows, 128), F32),
            pltpu.VMEM((dps, pad_rows, 128), BF16),
            pltpu.VMEM((dps, pad_rows, 128), BF16),
            pltpu.SemaphoreType.DMA((10,)),
            pltpu.SemaphoreType.DMA((2, 1)),
            pltpu.SemaphoreType.DMA((2, dps)),
            pltpu.SemaphoreType.DMA((2, pairs * dps)),
            pltpu.SemaphoreType.DMA((2, pairs * dps)),
            pltpu.SemaphoreType.DMA((2, dps)),
            pltpu.SemaphoreType.DMA((2, dps)),
            pltpu.SemaphoreType.DMA((2, dps)),
        ],
        compiler_params=pltpu.CompilerParams(
            collective_id=0, has_side_effects=True, vmem_limit_bytes=64 * 1024 * 1024 - 256 * 1024
        ),
    )(
        fine[0].reshape(strip_len, side * side, channels),
        jnp.asarray(tap_selector(side), BF16),
        conv_weight.reshape(3, 9 * channels, channels),
        query_weight,
        out_weight,
        coarse_kv[0].reshape(tiles * 16, inner),
        key_bias[0].T,
        zone_ids[0].reshape(1, slots),
        zone_counts[:, :1],
        grad_out[0].reshape(rows, channels),
    )
    weight_grads = weight_out.reshape(-1)
    if not reduce_here:
        weight_grads = lax.psum_scatter(
            weight_grads, ("dp", "sub", "rep"), scatter_dimension=0, tiled=True
        )
    return (weight_grads, tile_out.reshape(1, tiles, 2, 8, inner))


def solution(mesh):
    in_specs = (
        P(("grp", "dp", "rep"), "sub", None, None, None),
        P(),
        P(),
        P(),
        P(("grp", "sub", "rep"), "dp", None, None, None),
        P(("grp", "sub", "rep"), "dp", None),
        P(("grp", "dp", "rep"), "sub", None),
        P(("grp", "dp", "rep"), "sub"),
        P(("grp", "dp", "rep"), "sub", None, None, None),
    )
    out_specs = (P(("grp", "dp", "sub", "rep")), P(("grp", "sub", "rep"), "dp", None, None, None))
    return jax.shard_map(
        per_device, mesh=mesh, in_specs=in_specs, out_specs=out_specs, check_vma=False
    )
```

```python
import functools

import jax
import jax.numpy as jnp
import numpy as np
from jax import lax
from jax.experimental import pallas as pl
from jax.experimental.pallas import tpu as pltpu
from jax.sharding import PartitionSpec as P

HEADS = 8
MESH = pl.DeviceIdType.MESH
F32 = jnp.float32
BF16 = jnp.bfloat16


def dot(a, b):
    return jnp.dot(a, b, preferred_element_type=F32)


def dot_nt(a, b):
    return lax.dot_general(a, b, (((1,), (1,)), ((), ())), preferred_element_type=F32)


def dot_tn(a, b):
    return lax.dot_general(a, b, (((0,), (0,)), ((), ())), preferred_element_type=F32)


def iota(shape, dim):
    return lax.broadcasted_iota(jnp.int32, shape, dim)


def tap_selector(side):
    half = side // 2
    sel = np.zeros((9, half, half, side, side), np.float32)
    for b in range(3):
        for c in range(3):
            for y in range(half):
                for z in range(half):
                    yy, zz = 2 * y + b - 1, 2 * z + c - 1
                    if yy >= 0 and zz >= 0:
                        sel[b * 3 + c, y, z, yy, zz] = 1.0
    return sel.reshape(9 * half * half, side * side)


def kernel(
    cfg,
    fine_hbm,
    selector_hbm,
    conv_w_hbm,
    query_w_hbm,
    out_w_hbm,
    kv_hbm,
    bias_hbm,
    ids_hbm,
    count_hbm,
    upstream_hbm,
    weight_out,
    tile_out,
    fine,
    selector,
    conv_w,
    query_w,
    out_w,
    kv,
    bias_in,
    ids_in,
    count_in,
    upstream,
    meta,
    halo,
    t_even,
    t_odd,
    pre,
    feat,
    query,
    grad_att,
    grad_query,
    acc,
    metas,
    kv_send,
    kv_recv,
    slot_send,
    slot_recv,
    picks,
    rep_send,
    rep_recv,
    sub_send,
    sub_recv,
    part,
    dp_send,
    dp_recv,
    load_sem,
    halo_sem,
    meta_sem,
    kv_sem,
    slot_sem,
    rep_sem,
    sub_sem,
    dp_sem,
):
    dps, subs, tiles, cap, slots, rows_dev, reduce_here = cfg
    me = lax.axis_index("dp")
    sub = lax.axis_index("sub")
    rep = lax.axis_index("rep")
    cap_rows = cap * 16
    planes = t_even.shape[0]
    cells = t_even.shape[1]
    channels = fine.shape[2]
    lanes = slots * 8
    pairs = query.shape[1] // 128
    place_rows = dps * cap_rows
    peers = [lax.rem(me + d, dps) for d in range(dps)]

    barrier = pltpu.get_barrier_semaphore()
    greeted = 0
    for d in range(1, dps):
        pl.semaphore_signal(barrier, inc=1, device_id={"dp": peers[d]}, device_id_type=MESH)
        greeted += 1
    for step in (1, subs - 1) if subs > 2 else (1,):
        pl.semaphore_signal(
            barrier, inc=1, device_id={"sub": lax.rem(sub + step, subs)}, device_id_type=MESH
        )
        greeted += 1
    pl.semaphore_signal(barrier, inc=1, device_id={"rep": 1 - rep}, device_id_type=MESH)
    greeted += 1

    loads = []
    for i, (src, dst) in enumerate(
        (
            (ids_hbm, ids_in),
            (bias_hbm, bias_in),
            (count_hbm, count_in),
            (selector_hbm, selector),
            (fine_hbm, fine),
            (kv_hbm, kv),
            (upstream_hbm, upstream),
            (out_w_hbm, out_w),
            (conv_w_hbm, conv_w),
            (query_w_hbm, query_w),
        )
    ):
        copy = pltpu.make_async_copy(src, dst, load_sem.at[i])
        copy.start()
        loads.append(copy)

    def send(src, dst, sems, index, where):
        return pltpu.make_async_remote_copy(
            src_ref=src,
            dst_ref=dst,
            send_sem=sems.at[0, index],
            recv_sem=sems.at[1, index],
            device_id=where,
            device_id_type=MESH,
        )

    for i in range(3):
        loads[i].wait()
    spread = jnp.where(iota((slots, lanes), 0) == iota((slots, lanes), 1) // 8, 1.0, 0.0)
    ids_row = dot(ids_in[...].astype(BF16), spread.astype(BF16))
    key_of = jnp.where(iota((8, lanes), 0) == iota((8, lanes), 1) % 8, 1.0, 0.0)
    meta[:tiles, :] = dot_tn(bias_in[...], key_of.astype(BF16))
    meta[tiles:, :] = jnp.broadcast_to(ids_row, (8, lanes))
    metas[me] = meta[...]
    count = count_in[...].astype(F32)

    pl.semaphore_wait(barrier, greeted)
    meta_copies = [
        send(meta, metas.at[me], meta_sem, d, {"dp": peers[d]}) for d in range(1, dps)
    ]
    for copy in meta_copies:
        copy.start()
    loads[3].wait()
    loads[4].wait()
    halo_copy = send(
        fine.at[2 * planes - 1], halo, halo_sem, 0, {"sub": lax.rem(sub + 1, subs)}
    )
    halo_copy.start()

    def spread_taps(found, target, index):
        for tap in range(9):
            target[index, :, tap * channels : (tap + 1) * channels] = found[
                tap * cells : (tap + 1) * cells
            ]

    def unfold(i, carry):
        pair = jnp.concatenate([fine[2 * i], fine[2 * i + 1]], axis=1)
        found = dot(selector[...], pair).astype(BF16)
        spread_taps(found[:, :channels], t_even, i)
        spread_taps(found[:, channels:], t_odd, i + 1)
        return carry

    early = planes // 2
    lax.fori_loop(0, early, unfold, 0)

    def slot_dest(ids_row):
        owner_row = jnp.floor(ids_row * (1.0 / tiles))
        owner_col = jnp.transpose(jnp.broadcast_to(owner_row, (lanes, lanes)))
        earlier = (iota((lanes, lanes), 0) // 8) < (iota((lanes, lanes), 1) // 8)
        same = jnp.where((owner_col == owner_row) & earlier, 1.0, 0.0)
        rank = jnp.sum(same, axis=0, keepdims=True) * 0.125
        return owner_row * cap + rank

    me_f = me.astype(F32)

    def picker(ids_row):
        dest = slot_dest(ids_row)
        slot_row = (iota((cap_rows, lanes), 0) // 16).astype(F32) + me_f * cap
        first = (iota((cap_rows, lanes), 1) % 8) == 0
        by_slot = jnp.where((slot_row == dest) & first, 1.0, 0.0).astype(BF16)
        tile_row = (iota((tiles * 16, lanes), 0) // 16).astype(F32) + me_f * tiles
        by_tile = jnp.where(tile_row == ids_row, 1.0, 0.0).astype(BF16)
        matched = dot_nt(by_slot, by_tile)
        unit = (iota(matched.shape, 0) % 16) == (iota(matched.shape, 1) % 16)
        return jnp.where(unit, matched, 0.0).astype(BF16)

    for copy in meta_copies:
        copy.wait()
    loads[5].wait()
    for p in range(dps):
        picks[p] = picker(metas[p, tiles : tiles + 1, :])
    kv_copies = []
    for j in range(pairs):
        cut = slice(j * 128, (j + 1) * 128)
        chosen = dot(picks[...].reshape(place_rows, tiles * 16), kv[:, cut]).astype(BF16)
        kv_send[j] = chosen.reshape(dps, cap_rows, 128)
        group = []
        for d in range(dps - 1, 0, -1):
            copy = send(
                kv_send.at[j, peers[d]],
                kv_recv.at[j, me],
                kv_sem,
                j * dps + d,
                {"dp": peers[d]},
            )
            copy.start()
            group.append(copy)
        kv_copies.append(group)
        kv_recv[j, me] = kv_send[j, me]

    lax.fori_loop(early, planes, unfold, 0)
    halo_copy.wait()
    edge = dot(selector[...], halo[...])
    edge = jnp.where(sub > 0, edge, 0.0).astype(BF16)
    spread_taps(edge, t_odd, 0)

    row_count = planes * cells

    def columns(a):
        if a == 1:
            return t_even[...].reshape(row_count, 9 * channels)
        start = a // 2
        return t_odd[start : start + planes].reshape(row_count, 9 * channels)

    for i in range(6, 10):
        loads[i].wait()
    value = dot(columns(0), conv_w[0]) + dot(columns(1), conv_w[1]) + dot(columns(2), conv_w[2])
    pre[...] = value
    feat[...] = (value * jax.nn.sigmoid(value)).astype(BF16)
    query[...] = dot(feat[...], query_w[...]).astype(BF16)
    grad_att[...] = dot_nt(upstream[...], out_w[...]).astype(BF16)

    ids_row = meta[tiles : tiles + 1, :]
    dest = slot_dest(ids_row)
    dest2 = jnp.concatenate([dest, dest], axis=1)
    row_i = iota((place_rows, 2 * lanes), 0)
    lane_i = iota((place_rows, 2 * lanes), 1)
    fits = ((row_i // 16).astype(F32) == dest2) & (
        (row_i % 16) == (lane_i // lanes) * 8 + lane_i % 8
    )
    placing = jnp.where(fits, 1.0, 0.0).astype(BF16)

    bias = jnp.zeros((1, lanes), F32)
    for owner in range(dps):
        tile_row = iota((tiles, lanes), 0).astype(F32) + float(owner * tiles)
        bias = bias + jnp.sum(
            jnp.where(tile_row == ids_row, metas[owner, :tiles, :], 0.0), axis=0, keepdims=True
        )
    lane_slot = (iota((1, lanes), 1) // 8).astype(F32)
    bias = jnp.where(lane_slot < count, bias, -jnp.inf)

    low = iota((lanes, 128), 1) < 64
    conv_rows = 27 * channels
    out_rows = conv_rows + pairs * channels
    slot_copies = []

    def start_slots(j):
        group = []
        for d in range(dps - 1, 0, -1):
            copy = send(
                slot_send.at[j, peers[d]],
                slot_recv.at[j, me],
                slot_sem,
                j * dps + d,
                {"dp": peers[d]},
            )
            copy.start()
            group.append(copy)
        slot_copies.append(group)

    for j in range(pairs):
        for copy in kv_copies[j]:
            copy.wait()
        if j == pairs - 1:
            for i in range(pairs - 1):
                start_slots(i)
        kv_pair = dot_tn(placing, kv_recv[j].reshape(place_rows, 128)).astype(BF16)
        cut = slice(j * 128, (j + 1) * 128)
        keys = kv_pair[:lanes]
        values = kv_pair[lanes:]
        none = jnp.zeros_like(keys)
        keys2 = jnp.concatenate(
            [jnp.where(low, keys, none), jnp.where(low, none, keys)], axis=0
        )
        values2 = jnp.concatenate(
            [jnp.where(low, values, none), jnp.where(low, none, values)], axis=0
        )
        q = query[:, cut]
        g = grad_att[:, cut]
        scores = dot_nt(q, keys2) * 0.125
        grad_prob = dot_nt(g, values2)
        probs = []
        gs = []
        for h in range(2):
            s = scores[:, h * lanes : (h + 1) * lanes] + bias
            e = jnp.exp(s - jnp.max(s, axis=1, keepdims=True))
            prob = e * (1.0 / jnp.sum(e, axis=1, keepdims=True))
            gp = grad_prob[:, h * lanes : (h + 1) * lanes]
            probs.append(prob.astype(BF16))
            gs.append((prob * (gp - jnp.sum(prob * gp, axis=1, keepdims=True))).astype(BF16))
        prob_b = jnp.concatenate(probs, axis=1)
        grad_s = jnp.concatenate(gs, axis=1)
        gv = dot_tn(prob_b, g)
        gk = dot_tn(grad_s, q) * 0.125
        grad_pair = jnp.concatenate(
            [
                jnp.where(low, gk[:lanes], gk[lanes:]).astype(BF16),
                jnp.where(low, gv[:lanes], gv[lanes:]).astype(BF16),
            ],
            axis=0,
        )
        slot_send[j] = dot(placing, grad_pair).astype(BF16).reshape(dps, cap_rows, 128)
        if j == pairs - 1:
            start_slots(j)
        slot_recv[j, me] = slot_send[j, me]
        attended = dot(prob_b, values2).astype(BF16)
        acc[out_rows + j * 128 : out_rows + (j + 1) * 128, :] = dot_tn(attended, upstream[...])
        gq = (dot(grad_s, keys2) * 0.125).astype(BF16)
        grad_query[:, cut] = gq
        acc[pl.ds(conv_rows + j, channels, stride=pairs), :] = dot_tn(feat[...], gq)

    grad_feat = upstream[...].astype(F32) + dot_nt(grad_query[...], query_w[...])
    v = pre[...]
    sig = jax.nn.sigmoid(v)
    grad_pre = (grad_feat * (sig * (1.0 + v * (1.0 - sig)))).astype(BF16)

    def conv_grad(a):
        acc[a * 9 * channels : (a + 1) * 9 * channels, :] = dot_tn(columns(a), grad_pre)

    def scatter_tiles(j):
        for copy in slot_copies[j]:
            copy.wait()
        tile_out[:, j * 128 : (j + 1) * 128] = dot_tn(
            picks[...].reshape(place_rows, tiles * 16), slot_recv[j].reshape(place_rows, 128)
        )

    if not reduce_here:
        for a in range(3):
            conv_grad(a)
        for j in range(pairs):
            scatter_tiles(j)
        weight_out[...] = acc[: weight_out.shape[0], :]
        return

    pad_rows = rep_send.shape[2]
    acc[acc.shape[0] - 8 :, :] = jnp.zeros((8, 128), F32)

    def chunk(p, s, r):
        start = pl.multiple_of(((p * subs + s) * 2 + r) * rows_dev, 8)
        return acc[pl.ds(start, pad_rows), :]

    rep_copies = [
        send(rep_send.at[p], rep_recv.at[p], rep_sem, p, {"rep": 1 - rep}) for p in range(dps)
    ]
    sub_copies = [
        send(sub_send.at[p], sub_recv.at[p], sub_sem, p, {"sub": 1 - sub}) for p in range(dps)
    ]

    def start_rep(p):
        rep_send[p, 0] = chunk(p, 1 - sub, 1 - rep).astype(BF16)
        rep_send[p, 1] = chunk(p, sub, 1 - rep).astype(BF16)
        rep_copies[p].start()

    def start_sub(p):
        rep_copies[p].wait()
        sub_send[p] = (chunk(p, 1 - sub, rep) + rep_recv[p, 0].astype(F32)).astype(BF16)
        sub_copies[p].start()
        part[p] = chunk(p, sub, rep) + rep_recv[p, 1].astype(F32)

    def start_dp(p):
        sub_copies[p].wait()
        part[p] = part[p] + sub_recv[p].astype(F32)

        @pl.when(me != p)
        def _():
            dp_send[p] = part[p].astype(BF16)
            d = lax.rem(p - me + dps, dps)
            send(dp_send.at[p], dp_recv.at[d], dp_sem, d, {"dp": p}).start()

    done_rep = done_sub = 0
    for a in range(3):
        conv_grad(a)
        ready = dps if a == 2 else (a + 1) * 9 * channels // (4 * rows_dev)
        if a > 0 and done_sub < done_rep:
            start_sub(done_sub)
            done_sub += 1
        while done_rep < ready:
            start_rep(done_rep)
            done_rep += 1
    late = list(range(done_sub, dps))[::-1]
    for p in late:
        start_sub(p)
    for p in list(range(done_sub)) + late:
        start_dp(p)
    for j in range(pairs):
        scatter_tiles(j)
    total = part[me]
    for d in range(1, dps):
        send(dp_send.at[peers[d]], dp_recv.at[d], dp_sem, d, {"dp": peers[d]}).wait()
        total = total + dp_recv[d].astype(F32)
    weight_out[...] = total[:rows_dev]


def hand_over(weight_in, tile_in, weight_out, tile_out, sems):
    copies = [
        pltpu.make_async_copy(tile_in, tile_out, sems.at[0]),
        pltpu.make_async_copy(weight_in, weight_out, sems.at[1]),
    ]
    for copy in copies:
        copy.start()
    for copy in copies:
        copy.wait()


def per_device(
    fine,
    conv_weight,
    query_weight,
    out_weight,
    coarse_kv,
    key_bias,
    zone_ids,
    zone_counts,
    grad_out,
):
    strip_len, side, _, channels = fine.shape[1:]
    inner = query_weight.shape[1]
    tiles = coarse_kv.shape[1]
    slots = zone_ids.shape[1] * zone_ids.shape[2]
    dps, subs, reps = lax.axis_size("dp"), lax.axis_size("sub"), lax.axis_size("rep")
    cap = 2 * slots // dps
    cap_rows = cap * 16
    lanes = slots * 8
    planes = strip_len // 2
    cells = (side // 2) ** 2
    rows = planes * cells
    weight_rows = (27 * channels * channels + 2 * channels * inner) // 128
    devices = dps * subs * reps
    reduce_here = subs == 2 and weight_rows % (8 * devices) == 0
    rows_dev = weight_rows // devices if reduce_here else 16
    pad_rows = -(-rows_dev // 16) * 16
    cfg = (dps, subs, tiles, cap, slots, rows_dev, reduce_here)
    weight_shape = (rows_dev, 128) if reduce_here else (weight_rows, 128)
    vmem = pl.BlockSpec(memory_space=pltpu.VMEM)
    pairs = inner // 128
    hbm = pl.BlockSpec(memory_space=pltpu.HBM)
    weight_out, tile_out = pl.pallas_call(
        functools.partial(kernel, cfg),
        out_shape=(
            jax.ShapeDtypeStruct(weight_shape, F32),
            jax.ShapeDtypeStruct((tiles * 16, inner), F32),
        ),
        in_specs=[hbm] * 10,
        out_specs=(vmem, vmem),
        scratch_shapes=[
            pltpu.VMEM((strip_len, side * side, channels), BF16),
            pltpu.VMEM((9 * cells, side * side), BF16),
            pltpu.VMEM((3, 9 * channels, channels), BF16),
            pltpu.VMEM((channels, inner), BF16),
            pltpu.VMEM((inner, channels), BF16),
            pltpu.VMEM((tiles * 16, inner), BF16),
            pltpu.VMEM((8, tiles), BF16),
            pltpu.VMEM((1, slots), jnp.int32),
            pltpu.VMEM((1, 1), jnp.int32),
            pltpu.VMEM((rows, channels), BF16),
            pltpu.VMEM((tiles + 8, lanes), F32),
            pltpu.VMEM((side * side, channels), BF16),
            pltpu.VMEM((planes, cells, 9 * channels), BF16),
            pltpu.VMEM((planes + 1, cells, 9 * channels), BF16),
            pltpu.VMEM((rows, channels), F32),
            pltpu.VMEM((rows, channels), BF16),
            pltpu.VMEM((rows, inner), BF16),
            pltpu.VMEM((rows, inner), BF16),
            pltpu.VMEM((rows, inner), BF16),
            pltpu.VMEM((weight_rows + 8, 128), F32),
            pltpu.VMEM((dps, tiles + 8, lanes), F32),
            pltpu.VMEM((pairs, dps, cap_rows, 128), BF16),
            pltpu.VMEM((pairs, dps, cap_rows, 128), BF16),
            pltpu.VMEM((pairs, dps, cap_rows, 128), BF16),
            pltpu.VMEM((pairs, dps, cap_rows, 128), BF16),
            pltpu.VMEM((dps, cap_rows, tiles * 16), BF16),
            pltpu.VMEM((dps, 2, pad_rows, 128), BF16),
            pltpu.VMEM((dps, 2, pad_rows, 128), BF16),
            pltpu.VMEM((dps, pad_rows, 128), BF16),
            pltpu.VMEM((dps, pad_rows, 128), BF16),
            pltpu.VMEM((dps, pad_rows, 128), F32),
            pltpu.VMEM((dps, pad_rows, 128), BF16),
            pltpu.VMEM((dps, pad_rows, 128), BF16),
            pltpu.SemaphoreType.DMA((10,)),
            pltpu.SemaphoreType.DMA((2, 1)),
            pltpu.SemaphoreType.DMA((2, dps)),
            pltpu.SemaphoreType.DMA((2, pairs * dps)),
            pltpu.SemaphoreType.DMA((2, pairs * dps)),
            pltpu.SemaphoreType.DMA((2, dps)),
            pltpu.SemaphoreType.DMA((2, dps)),
            pltpu.SemaphoreType.DMA((2, dps)),
        ],
        compiler_params=pltpu.CompilerParams(
            collective_id=0, has_side_effects=True, vmem_limit_bytes=64 * 1024 * 1024 - 256 * 1024
        ),
    )(
        fine[0].reshape(strip_len, side * side, channels),
        jnp.asarray(tap_selector(side), BF16),
        conv_weight.reshape(3, 9 * channels, channels),
        query_weight,
        out_weight,
        coarse_kv[0].reshape(tiles * 16, inner),
        key_bias[0].T,
        zone_ids[0].reshape(1, slots),
        zone_counts[:, :1],
        grad_out[0].reshape(rows, channels),
    )
    if reduce_here:
        weight_out, tile_out = pl.pallas_call(
            hand_over,
            out_shape=(
                jax.ShapeDtypeStruct(weight_shape, F32),
                jax.ShapeDtypeStruct((tiles * 16, inner), F32),
            ),
            in_specs=[hbm] * 2,
            out_specs=(hbm, hbm),
            scratch_shapes=[pltpu.SemaphoreType.DMA((2,))],
        )(weight_out, tile_out)
    weight_grads = weight_out.reshape(-1)
    if not reduce_here:
        weight_grads = lax.psum_scatter(
            weight_grads, ("dp", "sub", "rep"), scatter_dimension=0, tiled=True
        )
    return (weight_grads, tile_out.reshape(1, tiles, 2, 8, inner))


def solution(mesh):
    in_specs = (
        P(("grp", "dp", "rep"), "sub", None, None, None),
        P(),
        P(),
        P(),
        P(("grp", "sub", "rep"), "dp", None, None, None),
        P(("grp", "sub", "rep"), "dp", None),
        P(("grp", "dp", "rep"), "sub", None),
        P(("grp", "dp", "rep"), "sub"),
        P(("grp", "dp", "rep"), "sub", None, None, None),
    )
    out_specs = (P(("grp", "dp", "sub", "rep")), P(("grp", "sub", "rep"), "dp", None, None, None))
    return jax.shard_map(
        per_device, mesh=mesh, in_specs=in_specs, out_specs=out_specs, check_vma=False
    )
```
